32 devices in a mesh: energy: 8 (over y, x, core), mom: 4 (over z).
Axes of the slice: x: 2, y: 2, z: 4, core: 2. Of those that a mesh axis runs over, the one named last changes fastest.
Arguments:
- green: bfloat16 [4, 8, 4, 2, 128, 128], P('mom', 'energy'), may hold values from -6 to 6
- grad: bfloat16 [4, 4, 2, 2, 128, 128], P('mom'), may hold values from -0.375 to 0.375
- coupling: float32 [4, 4], replicated, may hold values from 0.05 to 0.3
- occupation: float32 [4], replicated, may hold values from 0.1 to 2
- offsets: int32 [4], replicated, may hold values from 1 to 4, as said below
- neighbours: int32 [4, 2], replicated, may hold values from 0 to 3
- qtable: int32 [4, 4], P('mom'), may hold values from 0 to 3
Outputs:
- sigma: float32 [4, 8, 4, 2, 128, 128], P('mom', 'energy')
The draws below stay inside these ranges and needn't reach their ends.
Inputs may be any that keep to these rules, and one draw needn't show every extreme that they name: `offsets`: some mode has offset 1 and some mode has offset 4.
All inputs are finite; a program needn't handle non-finite values.
Results may differ from the reference program's by a relative error of at most 0.0029.
Values may be sent and summed in bfloat16 or wider, within the bound.
A program may use at most 64 MiB of HBM per device.

```python
import math
import jax
import jax.numpy as jnp
from jax import lax

ORB = 128
CLUST = 4
MODES = 4
NBR = 2
MAXOFF = 4
K = 4
NE = 8


def draw_offsets(key, part):
    key = jax.random.fold_in(key, 11)
    first_key, second_key = jax.random.split(key)
    others = jax.random.randint(first_key, (MODES - 2,), 1, MAXOFF + 1).astype(jnp.int32)
    ends = jnp.array([1, MAXOFF], jnp.int32)
    values = jnp.concatenate([ends, others])
    order = jax.random.permutation(second_key, MODES)
    return values[order].astype(jnp.int32)


def draw_qtable(key, part):
    key = jax.random.fold_in(key, 23)
    return jax.random.randint(key, (K, K), 0, K).astype(jnp.int32)


def set_ends(values, key, low, top_value):
    dims = values.shape
    spot = [jax.random.randint(jax.random.fold_in(key, axis), (), 0, dims[axis]) for axis in range(len(dims))]
    values = values.at[tuple(spot)].set(low)
    longest = dims.index(max(dims))
    spot[longest] = (spot[longest] + 1) % dims[longest]
    return values.at[tuple(spot)].set(top_value)


def block_levels(own_key, dims, shards, least, high):
    def one(axis_at, shards_of):
        steps = jax.random.uniform(jax.random.fold_in(jax.random.fold_in(own_key, 6), axis_at), (shards_of,), jnp.float32, least / len(shards), high / len(shards))
        return jnp.repeat(jnp.exp(steps), dims[axis_at] // shards_of).reshape((-1,) + (1,) * (len(dims) - axis_at - 1))

    gain = one(*shards[0])
    for cut in shards[1:]:
        gain = gain * one(*cut)
    return gain


def centred(own_key, extent, spread, bound, pieces=(), kind=jnp.bfloat16):
    drawn = jax.random.normal(own_key, extent, jnp.float32) * spread
    if len(pieces) > 0:
        drawn = block_levels(own_key, extent, pieces, -0.22, 0.18) * drawn
    return jnp.clip(drawn, min=-bound, max=bound).astype(kind)


def setup_inputs(seed: int = 0) -> dict:
    arg_keys = jax.random.split(jax.random.key(seed), 8)
    return {
        "green": centred(arg_keys[0], (K, NE, CLUST, 2, ORB, ORB), 1.0, 6.0, ((0, 4), (1, 8))),
        "grad": centred(arg_keys[1], (K, CLUST, NBR, 2, ORB, ORB), (2 * ORB) ** -0.5, 0.375, ((0, 4),)),
        "coupling": jnp.clip(jnp.exp(jax.random.uniform(arg_keys[2], (K, MODES), jnp.float32, math.log(0.05), math.log(0.3))), 0.05, 0.3),
        "occupation": jnp.clip(jnp.exp(jax.random.uniform(arg_keys[3], (MODES,), jnp.float32, math.log(0.1), math.log(2.0))), 0.1, 2.0),
        "offsets": draw_offsets(jax.random.fold_in(arg_keys[7], 71), 0),
        "neighbours": set_ends(jax.random.randint(arg_keys[5], (CLUST, NBR), 0, CLUST), jax.random.fold_in(arg_keys[5], 1), 0, CLUST - 1).astype(jnp.int32),
        "qtable": draw_qtable(jax.random.fold_in(arg_keys[7], 71), 0),
    }


def energy_terms(blocks, grad, pick, weights):
    high = lax.Precision.HIGHEST
    chosen = jnp.einsum('csx,jxrab->jcsrab', pick, blocks.astype(jnp.float32), precision=high).astype(jnp.bfloat16).astype(jnp.float32)
    grad_re = grad[:, :, :, 0].astype(jnp.float32)
    grad_im = grad[:, :, :, 1].astype(jnp.float32)
    chosen_re = chosen[:, :, :, 0]
    chosen_im = chosen[:, :, :, 1]
    prod_re = jnp.einsum('kcsab,jcsbd->kjcsad', grad_re, chosen_re, precision=high) - jnp.einsum('kcsab,jcsbd->kjcsad', grad_im, chosen_im, precision=high)
    prod_im = jnp.einsum('kcsab,jcsbd->kjcsad', grad_re, chosen_im, precision=high) + jnp.einsum('kcsab,jcsbd->kjcsad', grad_im, chosen_re, precision=high)
    prod_re = prod_re.astype(jnp.bfloat16).astype(jnp.float32)
    prod_im = prod_im.astype(jnp.bfloat16).astype(jnp.float32)
    triple_re = jnp.einsum('kjcsad,kcsed->kjcsae', prod_re, grad_re, precision=high) + jnp.einsum('kjcsad,kcsed->kjcsae', prod_im, grad_im, precision=high)
    triple_im = jnp.einsum('kjcsad,kcsed->kjcsae', prod_im, grad_re, precision=high) - jnp.einsum('kjcsad,kcsed->kjcsae', prod_re, grad_im, precision=high)
    accum_re = jnp.einsum('kjn,kjcsae->kncae', weights, triple_re, precision=high)
    accum_im = jnp.einsum('kjn,kjcsae->kncae', weights, triple_im, precision=high)
    return jnp.stack([accum_re, accum_im], axis=3)


def reference(green, grad, coupling, occupation, offsets, neighbours, qtable):
    pick = (neighbours[:, :, None] == jnp.arange(CLUST, dtype=jnp.int32)[None, None, :]).astype(jnp.float32)
    weights = coupling[qtable]
    padded = jnp.zeros((K, NE + 2 * MAXOFF, CLUST, 2, ORB, ORB), jnp.float32)

    def step(energy, padded):
        blocks = lax.dynamic_index_in_dim(green, energy, 1, keepdims=False)
        accum = energy_terms(blocks, grad, pick, weights)
        for mode in range(MODES):
            term = accum[:, mode][:, None]
            upper = (energy + MAXOFF + offsets[mode]).astype(jnp.int32)
            lower = (energy + MAXOFF - offsets[mode]).astype(jnp.int32)
            zero = jnp.zeros((), jnp.int32)
            old = lax.dynamic_slice(padded, (zero, upper, zero, zero, zero, zero), term.shape)
            padded = lax.dynamic_update_slice(padded, old + (1.0 + occupation[mode]) * term, (zero, upper, zero, zero, zero, zero))
            old = lax.dynamic_slice(padded, (zero, lower, zero, zero, zero, zero), term.shape)
            padded = lax.dynamic_update_slice(padded, old + occupation[mode] * term, (zero, lower, zero, zero, zero, zero))
        return padded

    padded = lax.fori_loop(0, NE, step, padded)
    return padded[:, MAXOFF:MAXOFF + NE]
```

```python
import functools

import jax
import jax.numpy as jnp
from jax import lax
from jax.experimental import pallas as pl
from jax.experimental.pallas import tpu as pltpu
from jax.sharding import PartitionSpec as P

MAXOFF = 4
GROUP = 8
ROWS = 16
LANES = 128
MESH = pl.DeviceIdType.MESH


def kernel(
    momenta,
    groups,
    group,
    green,
    grad,
    coupling,
    occupation,
    offsets,
    neighbours,
    qtable,
    out,
    held,
    coeffs,
    mixer,
    mixed,
    summed,
    blocks,
    left,
    right,
    grad_sem,
    send_sem,
    recv_sem,
    low_sem,
    high_sem,
    halo_sem,
    coeff_send,
    coeff_recv,
    back_send,
    back_recv,
):
    halves = held.shape[0]
    parts = momenta * group
    clusters, per = summed.shape[:2]
    listed = blocks.shape[1]
    modes = occupation.shape[0]
    orbits = blocks.shape[3]
    energy = lax.axis_index("energy")
    mom = lax.axis_index("mom")
    team = energy // group
    rank = energy % group
    base = team * group
    mine = mom * group + rank

    grad_copy = pltpu.make_async_copy(grad, blocks, grad_sem)
    grad_copy.start()
    own_copy = pltpu.make_async_copy(
        green.at[mine], held.at[:, rank + MAXOFF, mom], recv_sem
    )
    own_copy.start()

    barrier = pltpu.get_barrier_semaphore()

    def greet(start, first, count):
        def step(index, carry):
            place = lax.rem(mine + index, parts)
            pl.semaphore_signal(
                barrier,
                inc=1,
                device_id=(start + place % group, place // group),
                device_id_type=MESH,
            )
            return carry

        lax.fori_loop(first, count, step, 0)

    greet(base, 1, parts)
    if groups > 1:

        @pl.when(team > 0)
        def _():
            greet(base - group, 0, parts)

        @pl.when(team < groups - 1)
        def _():
            greet(base + group, 0, parts)

    lane = lax.broadcasted_iota(jnp.int32, coeffs.shape[1:], 1) // ROWS
    line = lax.broadcasted_iota(jnp.int32, coeffs.shape[1:], 0)
    spread = line * (LANES // ROWS) + lane
    value = jnp.zeros(coeffs.shape[1:], jnp.float32)
    for side in range(2):
        for step in range(MAXOFF):
            distance = MAXOFF - step if side == 0 else step + 1
            factors = []
            for mode in range(modes):
                factor = occupation[mode] + (1.0 if side == 0 else 0.0)
                factors.append(jnp.where(offsets[mode] == distance, factor, 0.0))
            for j in range(momenta):
                weight = factors[0] * coupling[qtable[0, j], 0]
                for mode in range(1, modes):
                    weight = weight + factors[mode] * coupling[qtable[0, j], mode]
                place = (side * MAXOFF + step) * momenta + j
                value = jnp.where(spread == place, weight, value)
    coeffs[mom] = value

    empty = jnp.zeros((halves, MAXOFF) + held.shape[2:], held.dtype)
    if groups == 1:
        held[:, :MAXOFF] = empty
        held[:, group + MAXOFF :] = empty
    else:

        @pl.when(team == 0)
        def _():
            held[:, :MAXOFF] = empty

        @pl.when(team == groups - 1)
        def _():
            held[:, group + MAXOFF :] = empty

    pl.semaphore_wait(barrier, parts - 1)
    if groups > 1:

        @pl.when(team > 0)
        def _():
            pl.semaphore_wait(barrier, parts)

        @pl.when(team < groups - 1)
        def _():
            pl.semaphore_wait(barrier, parts)

    def coeff_copy(index):
        return pltpu.make_async_remote_copy(
            src_ref=coeffs.at[mom],
            dst_ref=coeffs.at[mom],
            send_sem=coeff_send.at[index],
            recv_sem=coeff_recv.at[index],
            device_id=(energy, lax.rem(mom + index, momenta)),
            device_id_type=MESH,
        )

    for index in range(1, momenta):
        coeff_copy(index).start()

    def spread_out(start, first, slot, sent, received):
        def step(index, carry):
            place = lax.rem(mine + index, parts)
            pltpu.make_async_remote_copy(
                src_ref=green.at[place],
                dst_ref=held.at[:, slot, mom],
                send_sem=sent,
                recv_sem=received,
                device_id=(start + place % group, place // group),
                device_id_type=MESH,
            ).start()
            return carry

        lax.fori_loop(first, parts, step, 0)

    spread_out(base, 1, rank + MAXOFF, send_sem, recv_sem)
    before = (rank < MAXOFF) & (team > 0)
    after = (rank >= group - MAXOFF) & (team < groups - 1)
    if groups > 1:

        @pl.when(before)
        def _():
            spread_out(base - group, 0, rank + group + MAXOFF, halo_sem, high_sem)

        @pl.when(after)
        def _():
            spread_out(base + group, 0, rank + MAXOFF - group, halo_sem, low_sem)

    grad_copy.wait()
    for cluster in range(clusters):
        for place in range(listed):
            real = blocks[cluster, place, 0]
            imag = blocks[cluster, place, 1]
            left[cluster, place, :orbits, :orbits] = real
            left[cluster, place, :orbits, orbits:] = -imag
            left[cluster, place, orbits:, :orbits] = imag
            left[cluster, place, orbits:, orbits:] = real
            right[cluster, place, :orbits, :orbits] = real
            right[cluster, place, :orbits, orbits:] = imag
            right[cluster, place, orbits:, :orbits] = -imag
            right[cluster, place, orbits:, orbits:] = real

    for index in range(1, momenta):
        coeff_copy(index).wait_recv()
    diagonal = lax.broadcasted_iota(jnp.int32, (ROWS, LANES), 0) == (
        lax.broadcasted_iota(jnp.int32, (ROWS, LANES), 1) % ROWS
    )
    per_side = MAXOFF * momenta * ROWS // LANES
    for k in range(momenta):
        for row in range(2 * per_side):
            full = jnp.where(
                diagonal,
                jnp.broadcast_to(coeffs[k, row : row + 1, :], (ROWS, LANES)),
                0.0,
            )
            high = full.astype(jnp.bfloat16)
            low = (full - high.astype(jnp.float32)).astype(jnp.bfloat16)
            side, column = row // per_side, row % per_side
            columns = slice(column * LANES, (column + 1) * LANES)
            mixer[side, k * ROWS : (k + 1) * ROWS, columns] = high
            mixer[side, (momenta + k) * ROWS : (momenta + k + 1) * ROWS, columns] = low

    arrived = held.at[:, pl.ds(MAXOFF, group)]
    pltpu.make_async_copy(arrived, arrived, recv_sem).wait()
    if groups > 1:

        @pl.when(team > 0)
        def _():
            halo = held.at[:, pl.ds(0, MAXOFF)]
            pltpu.make_async_copy(halo, halo, low_sem).wait()

        @pl.when(team < groups - 1)
        def _():
            halo = held.at[:, pl.ds(group + MAXOFF, MAXOFF)]
            pltpu.make_async_copy(halo, halo, high_sem).wait()

    home = summed.at[mine // per, mine % per]

    def mix(index, carry):
        target = lax.rem(rank + 1 + index, group)
        for half in range(halves):
            below = held[half, pl.ds(target, MAXOFF)]
            above = held[half, pl.ds(target + MAXOFF + 1, MAXOFF)]
            total = jnp.dot(
                mixer[0],
                below.reshape(MAXOFF * momenta * ROWS, LANES),
                preferred_element_type=jnp.float32,
            ) + jnp.dot(
                mixer[1],
                above.reshape(MAXOFF * momenta * ROWS, LANES),
                preferred_element_type=jnp.float32,
            )
            total = total[: momenta * ROWS] + total[momenta * ROWS :]
            mixed[target, :, half] = total.astype(jnp.bfloat16).reshape(
                momenta, ROWS, LANES
            )

        def send(k):
            pltpu.make_async_remote_copy(
                src_ref=mixed.at[target, k],
                dst_ref=home,
                send_sem=back_send,
                recv_sem=back_recv,
                device_id=(base + target, k),
                device_id_type=MESH,
            ).start()

        for step in range(1, momenta):
            send(lax.rem(mom + step, momenta))

        @pl.when(target != rank)
        def _():
            send(mom)

        return carry

    lax.fori_loop(0, group, mix, 0)
    pltpu.make_async_copy(mixed.at[rank, mom], home, back_recv).start()
    pltpu.make_async_copy(summed, summed, back_recv).wait()

    for cluster in range(clusters):
        total = None
        for place in range(listed):
            chosen = summed[neighbours[cluster, place]].reshape(2 * orbits, orbits)
            prod = jnp.dot(left[cluster, place], chosen, preferred_element_type=jnp.float32)
            high = prod.astype(jnp.bfloat16)
            low = (prod - high.astype(jnp.float32)).astype(jnp.bfloat16)
            both = jnp.concatenate(
                [
                    jnp.concatenate([high[:orbits], high[orbits:]], axis=1),
                    jnp.concatenate([low[:orbits], low[orbits:]], axis=1),
                ],
                axis=0,
            )
            triple = lax.dot_general(
                both,
                right[cluster, place],
                (((1,), (1,)), ((), ())),
                preferred_element_type=jnp.float32,
            )
            triple = triple[:orbits] + triple[orbits:]
            total = triple if total is None else total + triple
        out[cluster, 0] = total[:, :orbits]
        out[cluster, 1] = total[:, orbits:]

    for index in range(1, momenta):
        coeff_copy(index).wait_send()
    others = green.at[pl.ds(0, parts - 1)]
    pltpu.make_async_copy(others, others, send_sem).wait()
    pltpu.make_async_copy(others, others, back_send).wait()
    if groups > 1:

        @pl.when(before | after)
        def _():
            pltpu.make_async_copy(green, green, halo_sem).wait()


def shards(teams, group, green, grad, coupling, occupation, offsets, neighbours, qtable):
    momenta = coupling.shape[0]
    clusters, listed = neighbours.shape
    orbits = grad.shape[4]
    parts = momenta * group
    halves = clusters * 2 * orbits * orbits // (parts * ROWS * LANES)
    per = parts // clusters
    pieces = green.reshape(parts, halves, ROWS, LANES)
    vmem = pl.BlockSpec(memory_space=pltpu.VMEM)
    smem = pl.BlockSpec(memory_space=pltpu.SMEM)
    anywhere = pl.BlockSpec(memory_space=pl.ANY)
    dma = pltpu.SemaphoreType.DMA
    result = pl.pallas_call(
        functools.partial(kernel, momenta, teams, group),
        out_shape=jax.ShapeDtypeStruct((clusters, 2, orbits, orbits), jnp.float32),
        in_specs=[anywhere, anywhere, smem, smem, smem, smem, smem],
        out_specs=vmem,
        scratch_shapes=[
            pltpu.VMEM((halves, group + 2 * MAXOFF, momenta, ROWS, LANES), jnp.bfloat16),
            pltpu.VMEM((momenta, max(8, momenta), LANES), jnp.float32),
            pltpu.VMEM((2, 2 * momenta * ROWS, MAXOFF * momenta * ROWS), jnp.bfloat16),
            pltpu.VMEM((group, momenta, halves, ROWS, LANES), jnp.bfloat16),
            pltpu.VMEM((clusters, per, halves, ROWS, LANES), jnp.bfloat16),
            pltpu.VMEM(grad.shape[1:], jnp.bfloat16),
            pltpu.VMEM((clusters, listed, 2 * orbits, 2 * orbits), jnp.bfloat16),
            pltpu.VMEM((clusters, listed, 2 * orbits, 2 * orbits), jnp.bfloat16),
            dma,
            dma,
            dma,
            dma,
            dma,
            dma,
            dma((momenta,)),
            dma((momenta,)),
            dma,
            dma,
        ],
        compiler_params=pltpu.CompilerParams(
            collective_id=0, has_side_effects=True, vmem_limit_bytes=32 * 1024 * 1024
        ),
    )(pieces, grad[0], coupling, occupation, offsets, neighbours, qtable)
    return result[None, None]


def solution(mesh):
    count = mesh.shape["energy"]
    group = GROUP if count % GROUP == 0 else count
    in_specs = (
        P("mom", "energy", None, None, None, None),
        P("mom", None, None, None, None, None),
        P(),
        P(),
        P(),
        P(),
        P("mom", None),
    )
    out_specs = P("mom", "energy", None, None, None, None)
    return jax.shard_map(
        functools.partial(shards, count // group, group),
        mesh=mesh,
        in_specs=in_specs,
        out_specs=out_specs,
        check_vma=False,
    )
```

```python
import functools

import jax
import jax.numpy as jnp
from jax import lax
from jax.experimental import pallas as pl
from jax.experimental.pallas import tpu as pltpu
from jax.sharding import PartitionSpec as P

MAXOFF = 4
GROUP = 8
ROWS = 16
LANES = 128
MESH = pl.DeviceIdType.MESH


def kernel(
    momenta,
    groups,
    group,
    green,
    grad,
    coupling_hbm,
    occupation_hbm,
    offsets_hbm,
    neighbours_hbm,
    qtable_hbm,
    out,
    held,
    coeffs,
    mixer,
    mixed,
    summed,
    blocks,
    left,
    right,
    coupling,
    occupation,
    offsets,
    neighbours,
    qtable,
    small_sem,
    grad_sem,
    send_sem,
    recv_sem,
    low_sem,
    high_sem,
    halo_sem,
    coeff_send,
    coeff_recv,
    back_send,
    back_recv,
):
    halves = held.shape[0]
    parts = momenta * group
    clusters, per = summed.shape[:2]
    listed = blocks.shape[1]
    modes = occupation.shape[0]
    orbits = blocks.shape[3]
    energy = lax.axis_index("energy")
    mom = lax.axis_index("mom")
    team = energy // group
    rank = energy % group
    base = team * group
    mine = mom * group + rank

    small_copies = [
        pltpu.make_async_copy(source, target, small_sem.at[index])
        for index, (source, target) in enumerate(
            [
                (coupling_hbm, coupling),
                (occupation_hbm, occupation),
                (offsets_hbm, offsets),
                (qtable_hbm, qtable),
                (neighbours_hbm, neighbours),
            ]
        )
    ]
    for copy in small_copies:
        copy.start()
    grad_copy = pltpu.make_async_copy(grad, blocks, grad_sem)
    grad_copy.start()
    own_copy = pltpu.make_async_copy(
        green.at[mine], held.at[:, rank + MAXOFF, mom], recv_sem
    )
    own_copy.start()

    barrier = pltpu.get_barrier_semaphore()

    def greet(start, first, count):
        def step(index, carry):
            place = lax.rem(mine + index, parts)
            pl.semaphore_signal(
                barrier,
                inc=1,
                device_id=(start + place % group, place // group),
                device_id_type=MESH,
            )
            return carry

        lax.fori_loop(first, count, step, 0)

    greet(base, 1, parts)
    if groups > 1:

        @pl.when(team > 0)
        def _():
            greet(base - group, 0, parts)

        @pl.when(team < groups - 1)
        def _():
            greet(base + group, 0, parts)

    for copy in small_copies:
        copy.wait()
    lane = lax.broadcasted_iota(jnp.int32, coeffs.shape[1:], 1) // ROWS
    line = lax.broadcasted_iota(jnp.int32, coeffs.shape[1:], 0)
    spread = line * (LANES // ROWS) + lane
    value = jnp.zeros(coeffs.shape[1:], jnp.float32)
    for side in range(2):
        for step in range(MAXOFF):
            distance = MAXOFF - step if side == 0 else step + 1
            factors = []
            for mode in range(modes):
                factor = occupation[mode] + (1.0 if side == 0 else 0.0)
                factors.append(jnp.where(offsets[mode] == distance, factor, 0.0))
            for j in range(momenta):
                weight = factors[0] * coupling[qtable[0, j], 0]
                for mode in range(1, modes):
                    weight = weight + factors[mode] * coupling[qtable[0, j], mode]
                place = (side * MAXOFF + step) * momenta + j
                value = jnp.where(spread == place, weight, value)
    coeffs[mom] = value

    empty = jnp.zeros((halves, MAXOFF) + held.shape[2:], held.dtype)
    if groups == 1:
        held[:, :MAXOFF] = empty
        held[:, group + MAXOFF :] = empty
    else:

        @pl.when(team == 0)
        def _():
            held[:, :MAXOFF] = empty

        @pl.when(team == groups - 1)
        def _():
            held[:, group + MAXOFF :] = empty

    pl.semaphore_wait(barrier, parts - 1)
    if groups > 1:

        @pl.when(team > 0)
        def _():
            pl.semaphore_wait(barrier, parts)

        @pl.when(team < groups - 1)
        def _():
            pl.semaphore_wait(barrier, parts)

    def coeff_copy(index):
        return pltpu.make_async_remote_copy(
            src_ref=coeffs.at[mom],
            dst_ref=coeffs.at[mom],
            send_sem=coeff_send.at[index],
            recv_sem=coeff_recv.at[index],
            device_id=(energy, lax.rem(mom + index, momenta)),
            device_id_type=MESH,
        )

    for index in range(1, momenta):
        coeff_copy(index).start()

    def spread_out(start, first, slot, sent, received):
        def step(index, carry):
            place = lax.rem(mine + index, parts)
            pltpu.make_async_remote_copy(
                src_ref=green.at[place],
                dst_ref=held.at[:, slot, mom],
                send_sem=sent,
                recv_sem=received,
                device_id=(start + place % group, place // group),
                device_id_type=MESH,
            ).start()
            return carry

        lax.fori_loop(first, parts, step, 0)

    spread_out(base, 1, rank + MAXOFF, send_sem, recv_sem)
    before = (rank < MAXOFF) & (team > 0)
    after = (rank >= group - MAXOFF) & (team < groups - 1)
    if groups > 1:

        @pl.when(before)
        def _():
            spread_out(base - group, 0, rank + group + MAXOFF, halo_sem, high_sem)

        @pl.when(after)
        def _():
            spread_out(base + group, 0, rank + MAXOFF - group, halo_sem, low_sem)

    grad_copy.wait()
    for cluster in range(clusters):
        for place in range(listed):
            real = blocks[cluster, place, 0]
            imag = blocks[cluster, place, 1]
            left[cluster, place, :orbits, :orbits] = real
            left[cluster, place, :orbits, orbits:] = -imag
            left[cluster, place, orbits:, :orbits] = imag
            left[cluster, place, orbits:, orbits:] = real
            right[cluster, place, :orbits, :orbits] = real
            right[cluster, place, :orbits, orbits:] = imag
            right[cluster, place, orbits:, :orbits] = -imag
            right[cluster, place, orbits:, orbits:] = real

    for index in range(1, momenta):
        coeff_copy(index).wait_recv()
    diagonal = lax.broadcasted_iota(jnp.int32, (ROWS, LANES), 0) == (
        lax.broadcasted_iota(jnp.int32, (ROWS, LANES), 1) % ROWS
    )
    per_side = MAXOFF * momenta * ROWS // LANES
    for k in range(momenta):
        for row in range(2 * per_side):
            full = jnp.where(
                diagonal,
                jnp.broadcast_to(coeffs[k, row : row + 1, :], (ROWS, LANES)),
                0.0,
            )
            high = full.astype(jnp.bfloat16)
            low = (full - high.astype(jnp.float32)).astype(jnp.bfloat16)
            side, column = row // per_side, row % per_side
            columns = slice(column * LANES, (column + 1) * LANES)
            mixer[side, k * ROWS : (k + 1) * ROWS, columns] = high
            mixer[side, (momenta + k) * ROWS : (momenta + k + 1) * ROWS, columns] = low

    arrived = held.at[:, pl.ds(MAXOFF, group)]
    pltpu.make_async_copy(arrived, arrived, recv_sem).wait()
    if groups > 1:

        @pl.when(team > 0)
        def _():
            halo = held.at[:, pl.ds(0, MAXOFF)]
            pltpu.make_async_copy(halo, halo, low_sem).wait()

        @pl.when(team < groups - 1)
        def _():
            halo = held.at[:, pl.ds(group + MAXOFF, MAXOFF)]
            pltpu.make_async_copy(halo, halo, high_sem).wait()

    home = summed.at[mine // per, mine % per]

    def mix(index, carry):
        target = lax.rem(rank + 1 + index, group)
        for half in range(halves):
            below = held[half, pl.ds(target, MAXOFF)]
            above = held[half, pl.ds(target + MAXOFF + 1, MAXOFF)]
            total = jnp.dot(
                mixer[0],
                below.reshape(MAXOFF * momenta * ROWS, LANES),
                preferred_element_type=jnp.float32,
            ) + jnp.dot(
                mixer[1],
                above.reshape(MAXOFF * momenta * ROWS, LANES),
                preferred_element_type=jnp.float32,
            )
            total = total[: momenta * ROWS] + total[momenta * ROWS :]
            mixed[target, :, half] = total.astype(jnp.bfloat16).reshape(
                momenta, ROWS, LANES
            )

        def send(k):
            pltpu.make_async_remote_copy(
                src_ref=mixed.at[target, k],
                dst_ref=home,
                send_sem=back_send,
                recv_sem=back_recv,
                device_id=(base + target, k),
                device_id_type=MESH,
            ).start()

        for step in range(1, momenta):
            send(lax.rem(mom + step, momenta))

        @pl.when(target != rank)
        def _():
            send(mom)

        return carry

    lax.fori_loop(0, group, mix, 0)
    pltpu.make_async_copy(mixed.at[rank, mom], home, back_recv).start()
    pltpu.make_async_copy(summed, summed, back_recv).wait()

    for cluster in range(clusters):
        total = None
        for place in range(listed):
            chosen = summed[neighbours[place, cluster]].reshape(2 * orbits, orbits)
            prod = jnp.dot(left[cluster, place], chosen, preferred_element_type=jnp.float32)
            high = prod.astype(jnp.bfloat16)
            low = (prod - high.astype(jnp.float32)).astype(jnp.bfloat16)
            both = jnp.concatenate(
                [
                    jnp.concatenate([high[:orbits], high[orbits:]], axis=1),
                    jnp.concatenate([low[:orbits], low[orbits:]], axis=1),
                ],
                axis=0,
            )
            triple = lax.dot_general(
                both,
                right[cluster, place],
                (((1,), (1,)), ((), ())),
                preferred_element_type=jnp.float32,
            )
            triple = triple[:orbits] + triple[orbits:]
            total = triple if total is None else total + triple
        out[cluster, 0] = total[:, :orbits]
        out[cluster, 1] = total[:, orbits:]

    for index in range(1, momenta):
        coeff_copy(index).wait_send()
    others = green.at[pl.ds(0, parts - 1)]
    pltpu.make_async_copy(others, others, send_sem).wait()
    pltpu.make_async_copy(others, others, back_send).wait()
    if groups > 1:

        @pl.when(before | after)
        def _():
            pltpu.make_async_copy(green, green, halo_sem).wait()


def shards(teams, group, green, grad, coupling, occupation, offsets, neighbours, qtable):
    momenta = coupling.shape[0]
    clusters, listed = neighbours.shape
    orbits = grad.shape[4]
    parts = momenta * group
    halves = clusters * 2 * orbits * orbits // (parts * ROWS * LANES)
    per = parts // clusters
    pieces = green.reshape(parts, halves, ROWS, LANES)
    vmem = pl.BlockSpec(memory_space=pltpu.VMEM)
    anywhere = pl.BlockSpec(memory_space=pl.ANY)
    dma = pltpu.SemaphoreType.DMA
    result = pl.pallas_call(
        functools.partial(kernel, momenta, teams, group),
        out_shape=jax.ShapeDtypeStruct((clusters, 2, orbits, orbits), jnp.float32),
        in_specs=[anywhere] * 7,
        out_specs=vmem,
        scratch_shapes=[
            pltpu.VMEM((halves, group + 2 * MAXOFF, momenta, ROWS, LANES), jnp.bfloat16),
            pltpu.VMEM((momenta, max(8, momenta), LANES), jnp.float32),
            pltpu.VMEM((2, 2 * momenta * ROWS, MAXOFF * momenta * ROWS), jnp.bfloat16),
            pltpu.VMEM((group, momenta, halves, ROWS, LANES), jnp.bfloat16),
            pltpu.VMEM((clusters, per, halves, ROWS, LANES), jnp.bfloat16),
            pltpu.VMEM(grad.shape[1:], jnp.bfloat16),
            pltpu.VMEM((clusters, listed, 2 * orbits, 2 * orbits), jnp.bfloat16),
            pltpu.VMEM((clusters, listed, 2 * orbits, 2 * orbits), jnp.bfloat16),
            pltpu.SMEM(coupling.shape, jnp.float32),
            pltpu.SMEM(occupation.shape, jnp.float32),
            pltpu.SMEM(offsets.shape, jnp.int32),
            pltpu.SMEM(neighbours.shape[::-1], jnp.int32),
            pltpu.SMEM(qtable.shape, jnp.int32),
            dma((5,)),
            dma,
            dma,
            dma,
            dma,
            dma,
            dma,
            dma((momenta,)),
            dma((momenta,)),
            dma,
            dma,
        ],
        compiler_params=pltpu.CompilerParams(
            collective_id=0, has_side_effects=True, vmem_limit_bytes=60 * 1024 * 1024
        ),
    )(pieces, grad[0], coupling, occupation, offsets, neighbours.T, qtable)
    return result[None, None]


def solution(mesh):
    count = mesh.shape["energy"]
    group = GROUP if count % GROUP == 0 else count
    in_specs = (
        P("mom", "energy", None, None, None, None),
        P("mom", None, None, None, None, None),
        P(),
        P(),
        P(),
        P(),
        P("mom", None),
    )
    out_specs = P("mom", "energy", None, None, None, None)
    return jax.shard_map(
        functools.partial(shards, count // group, group),
        mesh=mesh,
        in_specs=in_specs,
        out_specs=out_specs,
        check_vma=False,
    )
```

```python
import functools

import jax
import jax.numpy as jnp
from jax import lax
from jax.experimental import pallas as pl
from jax.experimental.pallas import tpu as pltpu
from jax.sharding import PartitionSpec as P

MAXOFF = 4
GROUP = 8
ROWS = 16
LANES = 128
MESH = pl.DeviceIdType.MESH


def kernel(
    momenta,
    groups,
    group,
    green,
    grad,
    coupling_hbm,
    occupation_hbm,
    offsets_hbm,
    neighbours_hbm,
    qtable_hbm,
    out,
    held,
    coeffs,
    mixer,
    mixed,
    summed,
    blocks,
    left,
    right,
    coupling,
    occupation,
    offsets,
    neighbours,
    qtable,
    small_sem,
    grad_sem,
    send_sem,
    recv_sem,
    low_sem,
    high_sem,
    halo_sem,
    coeff_send,
    coeff_recv,
    back_send,
    back_recv,
):
    halves = held.shape[0]
    parts = momenta * group
    clusters, per = summed.shape[:2]
    listed = blocks.shape[1]
    modes = occupation.shape[0]
    orbits = blocks.shape[3]
    energy = lax.axis_index("energy")
    mom = lax.axis_index("mom")
    team = energy // group
    rank = energy % group
    base = team * group
    mine = mom * group + rank

    small_copies = [
        pltpu.make_async_copy(source, target, small_sem.at[index])
        for index, (source, target) in enumerate(
            [
                (coupling_hbm, coupling),
                (occupation_hbm, occupation),
                (offsets_hbm, offsets),
                (qtable_hbm, qtable),
                (neighbours_hbm, neighbours),
            ]
        )
    ]
    for copy in small_copies:
        copy.start()
    grad_copy = pltpu.make_async_copy(grad, blocks, grad_sem)
    grad_copy.start()
    own_copy = pltpu.make_async_copy(
        green.at[mine], held.at[:, rank + MAXOFF, mom], recv_sem
    )
    own_copy.start()

    barrier = pltpu.get_barrier_semaphore()

    def greet(start, first, count):
        def step(index, carry):
            place = lax.rem(mine + index, parts)
            pl.semaphore_signal(
                barrier,
                inc=1,
                device_id=(start + place % group, place // group),
                device_id_type=MESH,
            )
            return carry

        lax.fori_loop(first, count, step, 0)

    greet(base, 1, parts)
    if groups > 1:

        @pl.when(team > 0)
        def _():
            greet(base - group, 0, parts)

        @pl.when(team < groups - 1)
        def _():
            greet(base + group, 0, parts)

    for copy in small_copies:
        copy.wait()
    lane = lax.broadcasted_iota(jnp.int32, coeffs.shape[1:], 1) // ROWS
    line = lax.broadcasted_iota(jnp.int32, coeffs.shape[1:], 0)
    spread = line * (LANES // ROWS) + lane
    value = jnp.zeros(coeffs.shape[1:], jnp.float32)
    for side in range(2):
        for step in range(MAXOFF):
            distance = MAXOFF - step if side == 0 else step + 1
            factors = []
            for mode in range(modes):
                factor = occupation[mode] + (1.0 if side == 0 else 0.0)
                factors.append(jnp.where(offsets[mode] == distance, factor, 0.0))
            for j in range(momenta):
                weight = factors[0] * coupling[qtable[0, j], 0]
                for mode in range(1, modes):
                    weight = weight + factors[mode] * coupling[qtable[0, j], mode]
                place = (side * MAXOFF + step) * momenta + j
                value = jnp.where(spread == place, weight, value)
    coeffs[mom] = value

    empty = jnp.zeros((halves, MAXOFF) + held.shape[2:], held.dtype)
    if groups == 1:
        held[:, :MAXOFF] = empty
        held[:, group + MAXOFF :] = empty
    else:

        @pl.when(team == 0)
        def _():
            held[:, :MAXOFF] = empty

        @pl.when(team == groups - 1)
        def _():
            held[:, group + MAXOFF :] = empty

    pl.semaphore_wait(barrier, parts - 1)
    if groups > 1:

        @pl.when(team > 0)
        def _():
            pl.semaphore_wait(barrier, parts)

        @pl.when(team < groups - 1)
        def _():
            pl.semaphore_wait(barrier, parts)

    def coeff_copy(index):
        return pltpu.make_async_remote_copy(
            src_ref=coeffs.at[mom],
            dst_ref=coeffs.at[mom],
            send_sem=coeff_send.at[index],
            recv_sem=coeff_recv.at[index],
            device_id=(energy, lax.rem(mom + index, momenta)),
            device_id_type=MESH,
        )

    for index in range(1, momenta):
        coeff_copy(index).start()

    def spread_out(start, first, slot, sent, received):
        def step(index, carry):
            place = lax.rem(mine + index, parts)
            pltpu.make_async_remote_copy(
                src_ref=green.at[place],
                dst_ref=held.at[:, slot, mom],
                send_sem=sent,
                recv_sem=received,
                device_id=(start + place % group, place // group),
                device_id_type=MESH,
            ).start()
            return carry

        lax.fori_loop(first, parts, step, 0)

    spread_out(base, 1, rank + MAXOFF, send_sem, recv_sem)
    before = (rank < MAXOFF) & (team > 0)
    after = (rank >= group - MAXOFF) & (team < groups - 1)
    if groups > 1:

        @pl.when(before)
        def _():
            spread_out(base - group, 0, rank + group + MAXOFF, halo_sem, high_sem)

        @pl.when(after)
        def _():
            spread_out(base + group, 0, rank + MAXOFF - group, halo_sem, low_sem)

    grad_copy.wait()
    for cluster in range(clusters):
        for place in range(listed):
            real = blocks[cluster, place, 0]
            imag = blocks[cluster, place, 1]
            left[cluster, place, :orbits, :orbits] = real
            left[cluster, place, :orbits, orbits:] = -imag
            left[cluster, place, orbits:, :orbits] = imag
            left[cluster, place, orbits:, orbits:] = real
            right[cluster, place, :orbits, :orbits] = real
            right[cluster, place, :orbits, orbits:] = imag
            right[cluster, place, orbits:, :orbits] = -imag
            right[cluster, place, orbits:, orbits:] = real

    for index in range(1, momenta):
        coeff_copy(index).wait_recv()
    diagonal = lax.broadcasted_iota(jnp.int32, (ROWS, LANES), 0) == (
        lax.broadcasted_iota(jnp.int32, (ROWS, LANES), 1) % ROWS
    )
    per_side = MAXOFF * momenta * ROWS // LANES
    for k in range(momenta):
        for row in range(2 * per_side):
            full = jnp.where(
                diagonal,
                jnp.broadcast_to(coeffs[k, row : row + 1, :], (ROWS, LANES)),
                0.0,
            )
            high = full.astype(jnp.bfloat16)
            low = (full - high.astype(jnp.float32)).astype(jnp.bfloat16)
            side, column = row // per_side, row % per_side
            columns = slice(column * LANES, (column + 1) * LANES)
            mixer[side, k * ROWS : (k + 1) * ROWS, columns] = high
            mixer[side, (momenta + k) * ROWS : (momenta + k + 1) * ROWS, columns] = low

    arrived = held.at[:, pl.ds(MAXOFF, group)]
    pltpu.make_async_copy(arrived, arrived, recv_sem).wait()
    if groups > 1:

        @pl.when(team > 0)
        def _():
            halo = held.at[:, pl.ds(0, MAXOFF)]
            pltpu.make_async_copy(halo, halo, low_sem).wait()

        @pl.when(team < groups - 1)
        def _():
            halo = held.at[:, pl.ds(group + MAXOFF, MAXOFF)]
            pltpu.make_async_copy(halo, halo, high_sem).wait()

    home = summed.at[mine // per, mine % per]

    def mix(index, carry):
        target = lax.rem(rank + 1 + index, group)
        for half in range(halves):
            below = held[half, pl.ds(target, MAXOFF)]
            above = held[half, pl.ds(target + MAXOFF + 1, MAXOFF)]
            total = jnp.dot(
                mixer[0],
                below.reshape(MAXOFF * momenta * ROWS, LANES),
                preferred_element_type=jnp.float32,
            ) + jnp.dot(
                mixer[1],
                above.reshape(MAXOFF * momenta * ROWS, LANES),
                preferred_element_type=jnp.float32,
            )
            total = total[: momenta * ROWS] + total[momenta * ROWS :]
            mixed[target, :, half] = total.astype(jnp.bfloat16).reshape(
                momenta, ROWS, LANES
            )

        def send(k):
            pltpu.make_async_remote_copy(
                src_ref=mixed.at[target, k],
                dst_ref=home,
                send_sem=back_send,
                recv_sem=back_recv,
                device_id=(base + target, k),
                device_id_type=MESH,
            ).start()

        for step in range(1, momenta):
            send(lax.rem(mom + step, momenta))

        @pl.when(target != rank)
        def _():
            send(mom)

        return carry

    lax.fori_loop(0, group, mix, 0)
    pltpu.make_async_copy(mixed.at[rank, mom], home, back_recv).start()
    pltpu.make_async_copy(summed, summed, back_recv).wait()

    for cluster in range(clusters):
        total = None
        for place in range(listed):
            chosen = summed[neighbours[place, cluster]].reshape(2 * orbits, orbits)
            prod = jnp.dot(left[cluster, place], chosen, preferred_element_type=jnp.float32)
            high = prod.astype(jnp.bfloat16)
            low = (prod - high.astype(jnp.float32)).astype(jnp.bfloat16)
            both = jnp.concatenate(
                [
                    jnp.concatenate([high[:orbits], high[orbits:]], axis=1),
                    jnp.concatenate([low[:orbits], low[orbits:]], axis=1),
                ],
                axis=0,
            )
            triple = lax.dot_general(
                both,
                right[cluster, place],
                (((1,), (1,)), ((), ())),
                preferred_element_type=jnp.float32,
            )
            triple = triple[:orbits] + triple[orbits:]
            total = triple if total is None else total + triple
        out[cluster, 0] = total[:, :orbits]
        out[cluster, 1] = total[:, orbits:]

    for index in range(1, momenta):
        coeff_copy(index).wait_send()
    others = green.at[pl.ds(0, parts - 1)]
    pltpu.make_async_copy(others, others, send_sem).wait()
    pltpu.make_async_copy(others, others, back_send).wait()
    if groups > 1:

        @pl.when(before | after)
        def _():
            pltpu.make_async_copy(green, green, halo_sem).wait()


def shards(teams, group, green, grad, coupling, occupation, offsets, neighbours, qtable):
    momenta = coupling.shape[0]
    clusters, listed = neighbours.shape
    orbits = grad.shape[4]
    parts = momenta * group
    halves = clusters * 2 * orbits * orbits // (parts * ROWS * LANES)
    per = parts // clusters
    pieces = green.reshape(parts, halves, ROWS, LANES)
    vmem = pl.BlockSpec(memory_space=pltpu.VMEM)
    anywhere = pl.BlockSpec(memory_space=pl.ANY)
    dma = pltpu.SemaphoreType.DMA
    result = pl.pallas_call(
        functools.partial(kernel, momenta, teams, group),
        out_shape=pltpu.VMEM((clusters, 2, orbits, orbits), jnp.float32),
        in_specs=[anywhere] * 7,
        out_specs=vmem,
        scratch_shapes=[
            pltpu.VMEM((halves, group + 2 * MAXOFF, momenta, ROWS, LANES), jnp.bfloat16),
            pltpu.VMEM((momenta, max(8, momenta), LANES), jnp.float32),
            pltpu.VMEM((2, 2 * momenta * ROWS, MAXOFF * momenta * ROWS), jnp.bfloat16),
            pltpu.VMEM((group, momenta, halves, ROWS, LANES), jnp.bfloat16),
            pltpu.VMEM((clusters, per, halves, ROWS, LANES), jnp.bfloat16),
            pltpu.VMEM(grad.shape[1:], jnp.bfloat16),
            pltpu.VMEM((clusters, listed, 2 * orbits, 2 * orbits), jnp.bfloat16),
            pltpu.VMEM((clusters, listed, 2 * orbits, 2 * orbits), jnp.bfloat16),
            pltpu.SMEM(coupling.shape, jnp.float32),
            pltpu.SMEM(occupation.shape, jnp.float32),
            pltpu.SMEM(offsets.shape, jnp.int32),
            pltpu.SMEM(neighbours.shape[::-1], jnp.int32),
            pltpu.SMEM(qtable.shape, jnp.int32),
            dma((5,)),
            dma,
            dma,
            dma,
            dma,
            dma,
            dma,
            dma((momenta,)),
            dma((momenta,)),
            dma,
            dma,
        ],
        compiler_params=pltpu.CompilerParams(
            collective_id=0, has_side_effects=True, vmem_limit_bytes=60 * 1024 * 1024
        ),
    )(pieces, grad[0], coupling, occupation, offsets, neighbours.T, qtable)
    return result[None, None]


def solution(mesh):
    count = mesh.shape["energy"]
    group = GROUP if count % GROUP == 0 else count
    in_specs = (
        P("mom", "energy", None, None, None, None),
        P("mom", None, None, None, None, None),
        P(),
        P(),
        P(),
        P(),
        P("mom", None),
    )
    out_specs = P("mom", "energy", None, None, None, None)
    return jax.shard_map(
        functools.partial(shards, count // group, group),
        mesh=mesh,
        in_specs=in_specs,
        out_specs=out_specs,
        check_vma=False,
    )
```
